32 devices in a mesh: seq: 8 (over z, y), head: 4 (over x, core).
Axes of the slice: x: 2, y: 2, z: 4, core: 2. Of those that a mesh axis runs over, the one named last changes fastest.
Arguments:
- hidden_in: bfloat16 [16384, 1536], P('seq'), may hold values from -6 to 6
- norm_gain: float32 [1536], replicated, may hold values from 0.5 to 1.5
- w_z: bfloat16 [1536, 3072], P(None, 'head'), may hold values from -0.15625 to 0.15625
- w_x: bfloat16 [1536, 3072], P(None, 'head'), may hold values from -0.15625 to 0.15625
- w_bc: bfloat16 [1536, 2, 128], P(None, None, 'head'), may hold values from -0.15625 to 0.15625
- w_dt: bfloat16 [1536, 48], P(None, 'head'), may hold values from -0.15625 to 0.15625
- conv_x: float32 [4, 3072], P(None, 'head'), may hold values from -3 to 3
- conv_x_bias: float32 [3072], P('head'), may hold values from -1.8 to 1.8
- conv_bc: float32 [4, 2, 128], P(None, None, 'head'), may hold values from -3 to 3
- conv_bc_bias: float32 [2, 128], P(None, 'head'), may hold values from -1.8 to 1.8
- dt_bias: float32 [48], P('head'), may hold values from -1.5 to 0.5
- a_log: float32 [48], P('head'), may hold values from -9 to -3.5
- d_skip: float32 [48], P('head'), may hold values from 0.5 to 1.5
- gate_gain: float32 [3072], P('head'), may hold values from 0.5 to 1.5
- w_out: bfloat16 [3072, 1536], P('head'), may hold values from -0.109375 to 0.109375
- out_grad: bfloat16 [16384, 1536], P(('seq', 'head')), may hold values from -6 to 6
Outputs:
- output: bfloat16 [16384, 1536], P(('seq', 'head'))
- input_grad: float32 [16384, 1536], P(('seq', 'head'))
- norm_gain_grad: float32 [1536], replicated
- w_z_grad: float32 [1536, 3072], P(None, 'head')
- w_x_grad: float32 [1536, 3072], P(None, 'head')
- w_bc_grad: float32 [1536, 2, 128], P(None, None, 'head')
- w_dt_grad: float32 [1536, 48], P(None, 'head')
- conv_x_grad: float32 [4, 3072], P(None, 'head')
- conv_x_bias_grad: float32 [3072], P('head')
- conv_bc_grad: float32 [4, 2, 128], P(None, None, 'head')
- conv_bc_bias_grad: float32 [2, 128], P(None, 'head')
- dt_bias_grad: float32 [48], P('head')
- a_log_grad: float32 [48], P('head')
- d_skip_grad: float32 [48], P('head')
- gate_gain_grad: float32 [3072], P('head')
- w_out_grad: float32 [3072, 1536], P('head')
The draws below stay inside these ranges and needn't reach their ends.
All inputs are finite; a program needn't handle non-finite values.
Results may differ from the reference program's by a relative error of at most 0.038.
Values may be sent and summed in bfloat16 or wider, within the bound.
A program may use at most 192 MiB of HBM per device.

```python
import jax
import jax.numpy as jnp
from jax import lax

D = 1536
INNER = 3072
HEADS = 48
HEAD_DIM = 64
STATE = 128
CONV = 4
BLOCK = 256
SEQ_LEN = 16384


def steps_of(stream_key, extent, split, low, high):
    factor_of, own = 1.0, jax.random.fold_in(stream_key, 6)
    for position, parts in split:
        heights = jnp.exp(jax.random.uniform(jax.random.fold_in(own, position), (parts,), jnp.float32, low / len(split), high / len(split)))
        factor_of = factor_of * jnp.repeat(heights, extent[position] // parts).reshape([-1 if axis == position else 1 for axis in range(len(extent))])
    return factor_of


def noise(rng, extent, deviation, reach, cuts=(), held_as=jnp.bfloat16):
    values = jax.random.normal(rng, extent, jnp.float32) * deviation
    if len(cuts) > 0:
        values = steps_of(rng, extent, cuts, -0.22, 0.18) * values
    return jnp.clip(values, min=-reach, max=reach).astype(held_as)


def setup_inputs(seed: int = 0) -> dict:
    streams_of = jax.random.split(jax.random.key(seed), 17)
    hidden_in = noise(streams_of[0], (SEQ_LEN, D), 1.0, 6.0, ((0, 8),))
    norm_gain = jnp.clip(1.0 + 0.1 * jax.random.normal(streams_of[1], (D,), jnp.float32), 0.5, 1.5)
    w_z = noise(streams_of[2], (D, INNER), D ** -0.5, 0.15625, ((1, 4),))
    w_x = noise(streams_of[3], (D, INNER), D ** -0.5, 0.15625, ((1, 4),))
    w_bc = noise(streams_of[4], (D, 2, STATE), D ** -0.5, 0.15625, ((2, 4),))
    w_dt = noise(streams_of[5], (D, HEADS), D ** -0.5, 0.15625, ((1, 4),))
    conv_x = noise(streams_of[6], (CONV, INNER), CONV ** -0.5, 3.0, ((1, 4),), jnp.float32)
    conv_x_bias = noise(streams_of[7], (INNER,), 0.3, 1.8, ((0, 4),), jnp.float32)
    conv_bc = noise(streams_of[8], (CONV, 2, STATE), CONV ** -0.5, 3.0, ((2, 4),), jnp.float32)
    conv_bc_bias = noise(streams_of[9], (2, STATE), 0.3, 1.8, ((1, 4),), jnp.float32)
    dt_bias = jnp.clip(-1.5 + 2.0 * jax.random.uniform(streams_of[10], (HEADS,), jnp.float32) ** steps_of(streams_of[10], (HEADS,), ((0, 4),), -0.2, 0.2), -1.5, 0.5)
    a_log = jnp.clip(-9.0 + 5.5 * jax.random.uniform(streams_of[11], (HEADS,), jnp.float32) ** steps_of(streams_of[11], (HEADS,), ((0, 4),), -0.2, 0.2), -9.0, -3.5)
    d_skip = jnp.clip(0.5 + 1.0 * jax.random.uniform(streams_of[12], (HEADS,), jnp.float32) ** steps_of(streams_of[12], (HEADS,), ((0, 4),), -0.2, 0.2), 0.5, 1.5)
    gate_gain = jnp.clip(1.0 + 0.1 * jax.random.normal(streams_of[13], (INNER,), jnp.float32), 0.5, 1.5)
    w_out = noise(streams_of[14], (INNER, D), INNER ** -0.5, 0.109375, ((0, 4),))
    out_grad = noise(streams_of[15], (SEQ_LEN, D), 1.0, 6.0, ((0, 32),))
    return {"hidden_in": hidden_in, "norm_gain": norm_gain, "w_z": w_z, "w_x": w_x, "w_bc": w_bc, "w_dt": w_dt, "conv_x": conv_x, "conv_x_bias": conv_x_bias, "conv_bc": conv_bc, "conv_bc_bias": conv_bc_bias, "dt_bias": dt_bias, "a_log": a_log, "d_skip": d_skip, "gate_gain": gate_gain, "w_out": w_out, "out_grad": out_grad}


@jax.custom_vjp
def low(v):
    return lax.optimization_barrier(v.astype(jnp.bfloat16)).astype(jnp.float32)

@jax.custom_vjp
def low_back(v):
    return v

def low_keep(v):
    return (low(v), None)

def low_pass(kept, grad):
    return (grad,)

def back_keep(v):
    return (v, None)

def back_low(kept, grad):
    return (low(grad),)
low.defvjp(low_keep, low_pass)
low_back.defvjp(back_keep, back_low)
EPSILON = 1e-05
HIGHEST = lax.Precision.HIGHEST

def block_scan(state, values, keys_b, queries_c, widths, a_log):
    count = values.shape[0] // BLOCK

    def advance(carry, pieces):
        vals, keys, queries, steps = pieces
        decay = steps * -jnp.exp(a_log)
        cumul = jnp.cumsum(decay, axis=0)
        causal = (lax.broadcasted_iota(jnp.int32, (BLOCK, BLOCK), 0) >= lax.broadcasted_iota(jnp.int32, (BLOCK, BLOCK), 1))[:, :, None]
        spread = cumul[:, None, :] - cumul[None, :, :]
        weights = jnp.where(causal, jnp.exp(jnp.where(causal, spread, 0.0)), 0.0)
        scores = jnp.dot(queries, keys.T, precision=HIGHEST)
        mixing = scores[:, :, None] * weights * steps[None, :, :]
        result = jnp.einsum('tsh,shp->thp', mixing, vals, precision=HIGHEST)
        result = result + jnp.exp(cumul)[:, :, None] * jnp.einsum('tn,hpn->thp', queries, carry, precision=HIGHEST)
        tail = jnp.exp(cumul[-1][None, :] - cumul) * steps
        carry = jnp.exp(cumul[-1])[:, None, None] * carry + jnp.einsum('sh,shp,sn->hpn', tail, vals, keys, precision=HIGHEST)
        return (carry, result)
    pieces = (values.reshape((count, BLOCK) + values.shape[1:]), keys_b.reshape((count, BLOCK) + keys_b.shape[1:]), queries_c.reshape((count, BLOCK) + queries_c.shape[1:]), widths.reshape((count, BLOCK) + widths.shape[1:]))
    final, results = lax.scan(jax.checkpoint(advance), state, pieces)
    return (final, results.reshape(values.shape))

def causal_silu(source, kernel, bias):
    length = source.shape[0]
    padded = jnp.concatenate([jnp.zeros((CONV - 1,) + source.shape[1:], jnp.float32), source], 0)
    total = bias + kernel[0] * padded[0:length]
    for offset in range(1, CONV):
        total = total + kernel[offset] * padded[offset:offset + length]
    return jax.nn.silu(total)

def layer(hidden, norm_gain, w_z, w_x, w_bc, w_dt, conv_x, conv_x_bias, conv_bc, conv_bc_bias, dt_bias, a_log, d_skip, gate_gain, w_out):
    normed_in = low(hidden * lax.rsqrt(lax.optimization_barrier(jnp.mean(hidden * hidden, -1, keepdims=True)) + EPSILON) * norm_gain)
    proj_z = low(low_back(jnp.dot(normed_in, w_z, precision=HIGHEST)))
    proj_x = low(low_back(jnp.dot(normed_in, w_x, precision=HIGHEST)))
    proj_bc = low(low_back(jnp.einsum('td,dkn->tkn', normed_in, w_bc, precision=HIGHEST)))
    proj_dt = low(low_back(jnp.dot(normed_in, w_dt, precision=HIGHEST)))
    inner_act = low(causal_silu(proj_x, conv_x, conv_x_bias))
    bc_act = low(causal_silu(proj_bc, conv_bc, conv_bc_bias))
    widths = jax.nn.softplus(proj_dt + dt_bias)
    values = inner_act.reshape(SEQ_LEN, HEADS, HEAD_DIM)
    start = jnp.zeros((HEADS, HEAD_DIM, STATE), jnp.float32)
    final, mixed = block_scan(start, values, bc_act[:, 0], bc_act[:, 1], widths, a_log)
    mixed = mixed + d_skip[None, :, None] * values
    gated = mixed.reshape(SEQ_LEN, INNER) * jax.nn.silu(proj_z)
    normed_out = low(gated * lax.rsqrt(lax.optimization_barrier(jnp.mean(gated * gated, -1, keepdims=True)) + EPSILON) * gate_gain)
    return hidden + jnp.dot(normed_out, w_out, precision=HIGHEST)

def reference(hidden_in, norm_gain, w_z, w_x, w_bc, w_dt, conv_x, conv_x_bias, conv_bc, conv_bc_bias, dt_bias, a_log, d_skip, gate_gain, w_out, out_grad):
    inputs = [hidden_in, norm_gain, w_z, w_x, w_bc, w_dt, conv_x, conv_x_bias, conv_bc, conv_bc_bias, dt_bias, a_log, d_skip, gate_gain, w_out]
    inputs = [item.astype(jnp.float32) for item in inputs]
    result, layer_back = jax.vjp(layer, *inputs)
    grads = layer_back(out_grad.astype(jnp.float32))
    return (result.astype(jnp.bfloat16), grads[0], grads[1], grads[2], grads[3], grads[4], grads[5], grads[6], grads[7], grads[8], grads[9], grads[10], grads[11], grads[12], grads[13], grads[14])
```

```python
import functools

import jax
import jax.numpy as jnp
from jax import lax
from jax.experimental import pallas as pl
from jax.experimental.pallas import tpu as pltpu
from jax.sharding import PartitionSpec as P

INNER = 3072
HEAD_DIM = 64
CONV = 4
STATE = 128
LANES = 128
CHUNK = 256
HALF = 128
EPSILON = 1e-05
F32 = jnp.float32
BF16 = jnp.bfloat16
VMEM_LIMIT = 56 * 1024 * 1024


def dot(left, right, contract=((1,), (0,)), precision=None):
    return lax.dot_general(
        left, right, (contract, ((), ())), preferred_element_type=F32, precision=precision
    )


NT = ((1,), (1,))
TN = ((0,), (0,))


def spread(per_head, expander):
    high = per_head.astype(BF16)
    low = (per_head - high.astype(F32)).astype(BF16)
    return dot(high, expander) + dot(low, expander)


def gather_heads(wide, expander):
    high = wide.astype(BF16)
    low = (wide - high.astype(F32)).astype(BF16)
    return dot(high, expander, NT) + dot(low, expander, NT)


def triangle(rows, lower):
    row = lax.broadcasted_iota(jnp.int32, (rows, rows), 0)
    column = lax.broadcasted_iota(jnp.int32, (rows, rows), 1)
    return row >= column if lower else row <= column


def split_pair(pair):
    first = lax.broadcasted_iota(jnp.int32, pair.shape, 1) < HEAD_DIM
    zero = jnp.zeros_like(pair)
    return jnp.where(first, pair, zero), jnp.where(first, zero, pair)


def sigmoid(value):
    return 0.5 * jnp.tanh(0.5 * value) + 0.5


def convolve(padded, taps, bias, lanes):
    total = bias[:, lanes] + taps[0:1, lanes] * padded[pl.ds(5, CHUNK), lanes]
    for tap in range(1, CONV):
        total = total + taps[tap : tap + 1, lanes] * padded[pl.ds(5 + tap, CHUNK), lanes]
    return total


def slabs(width):
    return [pl.ds(start, LANES) for start in range(0, width, LANES)]


def local_state_kernel(
    x_raw, bc_raw, dt_raw, edge_x, edge_bc, conv_x, bias_x, conv_bc, bias_bc, dt_bias, rate, expander,
    x_act, bc_act, dt_out, cumul_out, packed, padded_x, padded_bc, state, total,
):
    step = pl.program_id(0)
    inner = x_raw.shape[1]

    @pl.when(step == 0)
    def _():
        padded_x[0:8] = edge_x[...].astype(F32)
        padded_bc[0:8] = edge_bc[...].astype(F32)
        state[...] = jnp.zeros_like(state)
        total[...] = jnp.zeros_like(total)

    @pl.when(step > 0)
    def _():
        padded_x[0:8] = padded_x[CHUNK : CHUNK + 8]
        padded_bc[0:8] = padded_bc[CHUNK : CHUNK + 8]

    padded_x[8:] = x_raw[...].astype(F32)
    padded_bc[8:] = bc_raw[...].astype(F32)
    for lanes in slabs(2 * STATE):
        conv = convolve(padded_bc, conv_bc, bias_bc, lanes)
        bc_act[:, lanes] = (conv * sigmoid(conv)).astype(BF16)
    steps = jax.nn.softplus(dt_raw[...].astype(F32) + dt_bias[...])
    cumul = dot(
        triangle(CHUNK, True).astype(F32), steps * rate[...], precision=lax.Precision.HIGHEST
    )
    dt_out[...] = steps
    cumul_out[...] = cumul
    last = cumul[CHUNK - 1 : CHUNK]
    tail = spread(steps * jnp.exp(last - cumul), expander[...])
    keys = bc_act[:, 0:STATE]
    decay = spread(jnp.exp(jnp.broadcast_to(last, (8, LANES))), expander[...])[0:1]
    for index, lanes in enumerate(slabs(inner)):
        conv = convolve(padded_x, conv_x, bias_x, lanes)
        act = (conv * sigmoid(conv)).astype(BF16)
        x_act[:, lanes] = act
        cut = slice(index * LANES, (index + 1) * LANES)
        weighted = (act.astype(F32) * tail[:, cut]).astype(BF16)
        state[:, lanes] = decay[:, cut] * state[:, lanes] + dot(keys, weighted, TN)
    total[...] += last

    @pl.when(step == pl.num_programs(0) - 1)
    def _():
        packed[0:STATE] = state[...].astype(BF16)
        whole = spread(jnp.broadcast_to(total[...], (16, LANES)), expander[...])
        high = whole.astype(BF16)
        low = (whole - high.astype(F32)).astype(BF16)
        row = lax.broadcasted_iota(jnp.int32, whole.shape, 0)
        packed[STATE : STATE + 16] = jnp.where(row == 0, high, low)


def forward_kernel(
    x_act, bc_act, dt_in, cumul_in, gate, d_normed, state_in, skip, gain, expander,
    mixed_out, sums, states, state, scores, mixing, squares, dots,
):
    step = pl.program_id(0)
    inner = x_act.shape[1]

    @pl.when(step == 0)
    def _():
        state[...] = state_in[...]

    states[0] = state[...].astype(BF16)
    keys, queries = bc_act[:, 0:STATE], bc_act[:, STATE : 2 * STATE]
    steps, cumul = dt_in[...], cumul_in[...]
    turned = cumul.T
    last = cumul[CHUNK - 1 : CHUNK]
    raw = dot(queries, keys, NT)
    keep = triangle(HALF, True)
    scores[0] = jnp.where(keep, raw[0:HALF, 0:HALF], 0.0)
    scores[1] = raw[HALF:, 0:HALF]
    scores[2] = jnp.where(keep, raw[HALF:, HALF:], 0.0)
    steps_wide = spread(steps, expander[...])
    tail = spread(jnp.exp(last - cumul), expander[...])
    reach = spread(jnp.exp(cumul), expander[...])
    decay = spread(jnp.exp(jnp.broadcast_to(last, (8, LANES))), expander[...])[0:1]
    for index, lanes in enumerate(slabs(inner)):
        cut = slice(index * LANES, (index + 1) * LANES)
        act = x_act[:, lanes].astype(F32)
        scaled = act * steps_wide[:, cut]
        low = scaled.astype(BF16)
        pair = split_pair(low)
        for part in range(2):
            head = 2 * index + part
            column = cumul[:, head : head + 1]
            row = turned[head : head + 1]
            base = part * CHUNK
            for block, (at, source) in enumerate(((0, 0), (1, 0), (1, 1))):
                gap = column[at * HALF : (at + 1) * HALF] - row[:, source * HALF : (source + 1) * HALF]
                weight = (scores[block] * jnp.exp(jnp.minimum(gap, 0.0))).astype(BF16)
                if at == 0:
                    mixing[0:HALF, part * HALF : (part + 1) * HALF] = weight
                else:
                    mixing[HALF:, base + source * HALF : base + (source + 1) * HALF] = weight
        upper = dot(
            mixing[0:HALF, 0:CHUNK], jnp.concatenate([pair[0][0:HALF], pair[1][0:HALF]], 0)
        )
        lower = dot(mixing[HALF:, :], jnp.concatenate([pair[0], pair[1]], 0))
        held = state[:, lanes]
        carried = dot(queries, held.astype(BF16)) * reach[:, cut]
        mixed = jnp.concatenate([upper, lower], 0) + carried + skip[:, lanes] * act
        state[:, lanes] = decay[:, cut] * held + dot(keys, (scaled * tail[:, cut]).astype(BF16), TN)
        mixed_low = mixed.astype(BF16)
        mixed_out[:, lanes] = mixed_low
        z = gate[:, lanes].astype(F32)
        gated = mixed_low.astype(F32) * (z * sigmoid(z))
        grad = d_normed[:, lanes].astype(F32) * gain[:, lanes]
        if index == 0:
            squares[...] = gated * gated
            dots[...] = gated * grad
        else:
            squares[...] += gated * gated
            dots[...] += gated * grad
    lane = lax.broadcasted_iota(jnp.int32, (CHUNK, LANES), 1)
    sums[...] = jnp.where(
        lane == 0,
        jnp.sum(squares[...], 1, keepdims=True),
        jnp.where(lane == 1, jnp.sum(dots[...], 1, keepdims=True), 0.0),
    )


def gate_kernel(
    mixed_in, gate, d_normed, sums, bc_act, cumul_in, gain, expander,
    normed_out, d_mixed, d_gate, gain_grad, packed, adjoint, gain_total,
):
    step = pl.program_id(0)
    inner = mixed_in.shape[1]

    @pl.when(step == 0)
    def _():
        adjoint[...] = jnp.zeros_like(adjoint)
        gain_total[...] = jnp.zeros_like(gain_total)

    queries = bc_act[:, STATE : 2 * STATE]
    cumul = cumul_in[...]
    last = cumul[CHUNK - 1 : CHUNK]
    reach = spread(jnp.exp(cumul), expander[...])
    decay = spread(jnp.exp(jnp.broadcast_to(last, (8, LANES))), expander[...])[0:1]
    inverse = lax.rsqrt(sums[:, 0:1] / INNER + EPSILON)
    factor = inverse * inverse * inverse * sums[:, 1:2] / INNER
    inverse = jnp.broadcast_to(inverse, (CHUNK, LANES))
    factor = jnp.broadcast_to(factor, (CHUNK, LANES))
    for index, lanes in enumerate(slabs(inner)):
        cut = slice(index * LANES, (index + 1) * LANES)
        mixed = mixed_in[:, lanes].astype(F32)
        z = gate[:, lanes].astype(F32)
        soft = sigmoid(z)
        silu = z * soft
        gated = mixed * silu
        scaled = d_normed[:, lanes].astype(F32) * inverse
        normed = gated * inverse
        normed_out[:, lanes] = (normed * gain[:, lanes]).astype(BF16)
        gain_total[0:1, lanes] += jnp.sum(scaled * gated, 0, keepdims=True)
        d_gated = scaled * gain[:, lanes] - gated * factor
        d_y = (d_gated * silu).astype(BF16)
        d_mixed[:, lanes] = d_y
        d_gate[:, lanes] = (d_gated * mixed * (soft + silu * (1.0 - soft))).astype(BF16)
        reached = (d_y.astype(F32) * reach[:, cut]).astype(BF16)
        adjoint[:, lanes] = decay[:, cut] * adjoint[:, lanes] + dot(queries, reached, TN)

    @pl.when(step == pl.num_programs(0) - 1)
    def _():
        packed[...] = adjoint[...].astype(BF16)
        gain_grad[...] = gain_total[...]


def backward_kernel(
    x_raw, x_before, bc_raw, bc_before, dt_raw, edge_x, edge_bc, bc_act, dt_in, cumul_in, mixed_in, d_mixed,
    states, final_state, adjoint_in, conv_x, bias_x, conv_bc, bias_bc, dt_bias, rate, skip, skip_heads, expander,
    d_x_raw, d_bc_raw, d_dt_raw, first_x, first_bc, conv_x_grad, conv_bc_grad, head_grads,
    padded_x, padded_bc, later_x, later_bc, adjoint, next_state, scores, mixing, d_scores,
    d_steps_total, d_cumul_total,
):
    step = pl.program_id(0)
    steps_here = pl.num_programs(0)
    inner = x_raw.shape[1]

    @pl.when(step == 0)
    def _():
        adjoint[...] = adjoint_in[...]
        next_state[...] = final_state[...]
        later_x[CHUNK : CHUNK + 8] = jnp.zeros((8, inner), F32)
        later_bc[CHUNK : CHUNK + 8] = jnp.zeros((8, 2 * STATE), F32)
        conv_x_grad[...] = jnp.zeros_like(conv_x_grad)
        conv_bc_grad[...] = jnp.zeros_like(conv_bc_grad)
        head_grads[...] = jnp.zeros_like(head_grads)

    @pl.when(step > 0)
    def _():
        later_x[CHUNK : CHUNK + 8] = later_x[0:8]
        later_bc[CHUNK : CHUNK + 8] = later_bc[0:8]

    @pl.when(step == steps_here - 1)
    def _():
        padded_x[0:8] = edge_x[...].astype(F32)
        padded_bc[0:8] = edge_bc[...].astype(F32)

    @pl.when(step < steps_here - 1)
    def _():
        padded_x[0:8] = x_before[...].astype(F32)[8:16]
        padded_bc[0:8] = bc_before[...].astype(F32)[8:16]

    padded_x[8:] = x_raw[...].astype(F32)
    padded_bc[8:] = bc_raw[...].astype(F32)

    keys, queries = bc_act[:, 0:STATE], bc_act[:, STATE : 2 * STATE]
    steps, cumul = dt_in[...], cumul_in[...]
    turned = cumul.T
    last = cumul[CHUNK - 1 : CHUNK]
    raw = dot(keys, queries, NT)
    keep = triangle(HALF, False)
    scores[0] = jnp.where(keep, raw[0:HALF, 0:HALF], 0.0)
    scores[1] = raw[0:HALF, HALF:]
    scores[2] = jnp.where(keep, raw[HALF:, HALF:], 0.0)
    d_scores[...] = jnp.zeros_like(d_scores)
    steps_wide = spread(steps, expander[...])
    tail = spread(jnp.exp(last - cumul), expander[...])
    reach = spread(jnp.exp(cumul), expander[...])
    decay = spread(jnp.exp(jnp.broadcast_to(last, (8, LANES))), expander[...])[0:1]
    d_keys = jnp.zeros((CHUNK, STATE), F32)
    d_queries = jnp.zeros((CHUNK, STATE), F32)
    d_steps = jnp.zeros((CHUNK, LANES), F32)
    d_mix_sum = jnp.zeros((CHUNK, LANES), F32)
    d_skip_sum = jnp.zeros((CHUNK, LANES), F32)
    ending = jnp.zeros((8, LANES), F32)
    for index, lanes in enumerate(slabs(inner)):
        cut = slice(index * LANES, (index + 1) * LANES)
        expand = expander[:, lanes]
        conv = convolve(padded_x, conv_x, bias_x, lanes)
        soft = sigmoid(conv)
        act = (conv * soft).astype(BF16).astype(F32)
        scaled = act * steps_wide[:, cut]
        low = scaled.astype(BF16)
        pair = split_pair(low)
        d_y_low = d_mixed[:, lanes]
        d_y = d_y_low.astype(F32)
        d_pair = split_pair(d_y_low)
        for part in range(2):
            head = 2 * index + part
            column = cumul[:, head : head + 1]
            row = turned[head : head + 1]
            base = part * CHUNK
            d_mixing = dot(pair[part], d_y_low, NT)
            for block, (source, at) in enumerate(((0, 0), (0, 1), (1, 1))):
                gap = row[:, at * HALF : (at + 1) * HALF] - column[source * HALF : (source + 1) * HALF]
                fade = jnp.exp(jnp.minimum(gap, 0.0))
                weight = (scores[block] * fade).astype(BF16)
                d_scores[block] += fade * d_mixing[
                    source * HALF : (source + 1) * HALF, at * HALF : (at + 1) * HALF
                ]
                if source == 0:
                    mixing[0:HALF, base + at * HALF : base + (at + 1) * HALF] = weight
                else:
                    mixing[HALF:, part * HALF : (part + 1) * HALF] = weight
        upper = dot(mixing[0:HALF, :], jnp.concatenate([d_pair[0], d_pair[1]], 0))
        lower = dot(
            mixing[HALF:, 0:CHUNK], jnp.concatenate([d_pair[0][HALF:], d_pair[1][HALF:]], 0)
        )
        after = adjoint[:, lanes]
        after_low = after.astype(BF16)
        before_low = states[0, :, lanes]
        u = jnp.concatenate([upper, lower], 0) + dot(keys, after_low) * tail[:, cut]
        d_act = steps_wide[:, cut] * u + skip[:, lanes] * d_y
        d_steps += gather_heads(act * u, expand)
        d_mix_sum += gather_heads(d_y * mixed_in[:, lanes].astype(F32), expand)
        d_skip_sum += gather_heads(d_y * act, expand)
        closing = jnp.sum(after * next_state[:, lanes].astype(F32), 0, keepdims=True)
        ending += gather_heads(jnp.broadcast_to(closing, (8, LANES)), expand)
        next_state[:, lanes] = before_low
        reached = (d_y * reach[:, cut]).astype(BF16)
        d_queries += dot(reached, before_low, NT)
        d_keys += dot((scaled * tail[:, cut]).astype(BF16), after_low, NT)
        adjoint[:, lanes] = decay[:, cut] * after + dot(queries, reached, TN)

        d_conv = d_act * (soft + conv * soft * (1.0 - soft))
        later_x[0:CHUNK, lanes] = d_conv
        back = conv_x[CONV - 1 : CONV, lanes] * d_conv
        for tap in range(CONV - 1):
            back = back + conv_x[tap : tap + 1, lanes] * later_x[pl.ds(CONV - 1 - tap, CHUNK), lanes]
        d_x_raw[:, lanes] = back.astype(BF16)
        for tap in range(CONV):
            conv_x_grad[tap : tap + 1, lanes] += jnp.sum(
                padded_x[pl.ds(5 + tap, CHUNK), lanes] * d_conv, 0, keepdims=True
            )
        conv_x_grad[CONV : CONV + 1, lanes] += jnp.sum(d_conv, 0, keepdims=True)

    d_scores[0] = jnp.where(keep, d_scores[0], 0.0)
    d_scores[2] = jnp.where(keep, d_scores[2], 0.0)
    corner, beside, end = (d_scores[block].astype(BF16) for block in range(3))
    d_keys += jnp.concatenate(
        [dot(jnp.concatenate([corner, beside], 1), queries), dot(end, queries[HALF:])], 0
    )
    d_queries += jnp.concatenate(
        [
            dot(corner, keys[0:HALF], TN),
            dot(jnp.concatenate([beside, end], 0), keys, TN),
        ],
        0,
    )
    for index, lanes in enumerate(slabs(2 * STATE)):
        conv = convolve(padded_bc, conv_bc, bias_bc, lanes)
        soft = sigmoid(conv)
        d_conv = (d_keys, d_queries)[index] * (soft + conv * soft * (1.0 - soft))
        later_bc[0:CHUNK, lanes] = d_conv
        back = conv_bc[CONV - 1 : CONV, lanes] * d_conv
        for tap in range(CONV - 1):
            back = back + conv_bc[tap : tap + 1, lanes] * later_bc[pl.ds(CONV - 1 - tap, CHUNK), lanes]
        d_bc_raw[:, lanes] = back.astype(BF16)
        for tap in range(CONV):
            conv_bc_grad[tap : tap + 1, lanes] += jnp.sum(
                padded_bc[pl.ds(5 + tap, CHUNK), lanes] * d_conv, 0, keepdims=True
            )
        conv_bc_grad[CONV : CONV + 1, lanes] += jnp.sum(d_conv, 0, keepdims=True)

    d_cumul = d_mix_sum - skip_heads[...] * d_skip_sum - steps * d_steps
    d_decay = (
        dot(triangle(CHUNK, False).astype(F32), d_cumul, precision=lax.Precision.HIGHEST) + ending[0:1]
    )
    pre = dt_raw[...].astype(F32) + dt_bias[...]
    d_pre = (d_steps + rate[...] * d_decay) * sigmoid(pre)
    d_dt_raw[...] = d_pre.astype(BF16)
    head_grads[0:1] += jnp.sum(d_pre, 0, keepdims=True)
    head_grads[1:2] += jnp.sum(d_decay * steps * rate[...], 0, keepdims=True)
    head_grads[2:3] += jnp.sum(d_skip_sum, 0, keepdims=True)

    @pl.when(step == steps_here - 1)
    def _():
        first_x[...] = later_x[0:8]
        first_bc[...] = later_bc[0:8]


def shape(extent, dtype):
    return jax.ShapeDtypeStruct(extent, dtype)


def whole(array):
    rank = array.ndim if hasattr(array, "ndim") else len(array.shape)
    return pl.BlockSpec(array.shape, lambda step: (0,) * rank)


def params():
    return pltpu.CompilerParams(
        dimension_semantics=("arbitrary",), vmem_limit_bytes=VMEM_LIMIT
    )


def cost(flops, moved):
    return pl.CostEstimate(flops=int(flops), bytes_accessed=int(moved), transcendentals=0)


def by_chunk(width, turn, block=0):
    return pl.BlockSpec((CHUNK, width), lambda step: (turn(step), block))


def from_behind(value, axis, by):
    size = lax.axis_size(axis)
    pairs = [(i, i + by) for i in range(size) if 0 <= i + by < size]
    return lax.ppermute(value, axis, pairs)


def transposed_times(left, right):
    return dot(left, right, TN)


def per_device(
    hidden_in,
    norm_gain,
    w_z,
    w_x,
    w_bc,
    w_dt,
    conv_x,
    conv_x_bias,
    conv_bc,
    conv_bc_bias,
    dt_bias,
    a_log,
    d_skip,
    gate_gain,
    w_out,
    out_grad,
):
    tokens, width = hidden_in.shape
    own_rows = out_grad.shape[0]
    heads_here = w_dt.shape[1]
    inner = w_z.shape[1]
    states_here = w_bc.shape[2]
    chunks = tokens // CHUNK
    ahead = lambda step: step
    behind = lambda step: chunks - 1 - step
    seq_size = lax.axis_size("seq")
    seq_index = lax.axis_index("seq")
    first_row = lax.axis_index("head") * own_rows

    def lane_row(vector):
        return jnp.pad(vector, (0, LANES - heads_here))[None, :]

    piece = lax.all_gather(out_grad, "head", axis=0, tiled=True)
    w_bc_parts = lax.all_gather(w_bc.reshape(width, 2 * states_here), "head")
    small_parts = lax.all_gather(
        jnp.concatenate([conv_bc, conv_bc_bias[None]], 0).reshape((CONV + 1) * 2, states_here), "head"
    )
    w_bc_all = (
        w_bc_parts.reshape(-1, width, 2, states_here).transpose(1, 2, 0, 3).reshape(width, 2 * STATE)
    )
    small = (
        small_parts.reshape(-1, CONV + 1, 2, states_here).transpose(1, 2, 0, 3).reshape(CONV + 1, 2 * STATE)
    )
    conv_bc_all, bias_bc_all = small[0:CONV], small[CONV:]
    w_dt_wide = jnp.pad(w_dt, ((0, 0), (0, LANES - heads_here)))
    dt_bias_row = lane_row(dt_bias)
    rate = lane_row(-jnp.exp(a_log))
    skip_heads = lane_row(d_skip)
    skip = jnp.repeat(d_skip, HEAD_DIM)[None, :]
    gain = gate_gain[None, :]
    bias_x = conv_x_bias[None, :]
    expander = (
        lax.broadcasted_iota(jnp.int32, (LANES, inner), 0)
        == lax.broadcasted_iota(jnp.int32, (LANES, inner), 1) // HEAD_DIM
    ).astype(BF16)

    hidden_f = hidden_in.astype(F32)
    normed_in = (
        hidden_f * lax.rsqrt(jnp.mean(hidden_f * hidden_f, -1, keepdims=True) + EPSILON) * norm_gain
    ).astype(BF16)
    proj_x = dot(normed_in, w_x).astype(BF16)
    proj_bc = dot(normed_in, w_bc_all).astype(BF16)
    proj_dt = dot(normed_in, w_dt_wide).astype(BF16)
    edge_x, edge_bc = from_behind((proj_x[-8:], proj_bc[-8:]), "seq", 1)
    proj_z = dot(normed_in, w_z).astype(BF16)

    wide = by_chunk(inner, ahead)
    lanes_f = by_chunk(LANES, ahead)
    pair_spec = by_chunk(2 * STATE, ahead)
    x_act, bc_act, steps, cumul, packed = pl.pallas_call(
        local_state_kernel,
        grid=(chunks,),
        in_specs=[wide, pair_spec, lanes_f]
        + [whole(a) for a in (edge_x, edge_bc, conv_x, bias_x, conv_bc_all, bias_bc_all)]
        + [whole(a) for a in (dt_bias_row, rate, expander)],
        out_specs=[
            wide, pair_spec, lanes_f, lanes_f,
            pl.BlockSpec((STATE + 16, inner), lambda step: (0, 0)),
        ],
        out_shape=[
            shape((tokens, inner), BF16),
            shape((tokens, 2 * STATE), BF16),
            shape((tokens, LANES), F32),
            shape((tokens, LANES), F32),
            shape((STATE + 16, inner), BF16),
        ],
        scratch_shapes=[
            pltpu.VMEM((CHUNK + 8, inner), F32),
            pltpu.VMEM((CHUNK + 8, 2 * STATE), F32),
            pltpu.VMEM((STATE, inner), F32),
            pltpu.VMEM((1, LANES), F32),
        ],
        compiler_params=params(),
        cost_estimate=cost(1.5e9, 20e6),
        name="local_state",
    )(
        proj_x, proj_bc, proj_dt, edge_x, edge_bc, conv_x, bias_x, conv_bc_all, bias_bc_all,
        dt_bias_row, rate, expander,
    )

    gathered = lax.all_gather(packed, "seq")
    d_normed = dot(piece, w_out, NT).astype(BF16)
    totals = gathered[:, STATE].astype(F32) + gathered[:, STATE + 1].astype(F32)
    place = jnp.arange(seq_size)
    between = (place[None, :] > place[:, None]) & (place[None, :] < seq_index)
    since = jnp.sum(jnp.where(between[:, :, None], totals[None], 0.0), 1)
    weight_in = jnp.where((place < seq_index)[:, None], jnp.exp(since), 0.0)
    state_in = jnp.sum(weight_in[:, None, :] * gathered[:, 0:STATE].astype(F32), 0)
    until = (place[None, :] < place[:, None]) & (place[None, :] > seq_index)
    ahead_of = jnp.sum(jnp.where(until[:, :, None], totals[None], 0.0), 1)
    weight_back = jnp.where((place > seq_index)[:, None], jnp.exp(ahead_of), 0.0)
    final_state = (jnp.exp(totals[seq_index])[None] * state_in + packed[0:STATE].astype(F32)).astype(BF16)

    mixed, sums, states = pl.pallas_call(
        forward_kernel,
        grid=(chunks,),
        in_specs=[wide, pair_spec, lanes_f, lanes_f, wide, wide]
        + [whole(a) for a in (state_in, skip, gain, expander)],
        out_specs=[wide, lanes_f, pl.BlockSpec((1, STATE, inner), lambda step: (step, 0, 0))],
        out_shape=[
            shape((tokens, inner), BF16),
            shape((tokens, LANES), F32),
            shape((chunks, STATE, inner), BF16),
        ],
        scratch_shapes=[
            pltpu.VMEM((STATE, inner), F32),
            pltpu.VMEM((3, HALF, HALF), F32),
            pltpu.VMEM((CHUNK, 2 * CHUNK), BF16),
            pltpu.VMEM((CHUNK, LANES), F32),
            pltpu.VMEM((CHUNK, LANES), F32),
        ],
        compiler_params=params(),
        cost_estimate=cost(10e9, 20e6),
        name="forward_scan",
    )(x_act, bc_act, steps, cumul, proj_z, d_normed, state_in, skip, gain, expander)

    sums = lax.psum(sums[:, 0:2], "head")

    wide_r = by_chunk(inner, behind)
    lanes_r = by_chunk(LANES, behind)
    pair_r = by_chunk(2 * STATE, behind)
    normed_out, d_mixed, grad_z, gain_grad, adjoint_packed = pl.pallas_call(
        gate_kernel,
        grid=(chunks,),
        in_specs=[wide_r, wide_r, wide_r, by_chunk(2, behind), pair_r, lanes_r]
        + [whole(a) for a in (gain, expander)],
        out_specs=[
            wide_r, wide_r, wide_r,
            pl.BlockSpec((8, inner), lambda step: (0, 0)),
            pl.BlockSpec((STATE, inner), lambda step: (0, 0)),
        ],
        out_shape=[
            shape((tokens, inner), BF16),
            shape((tokens, inner), BF16),
            shape((tokens, inner), BF16),
            shape((8, inner), F32),
            shape((STATE, inner), BF16),
        ],
        scratch_shapes=[pltpu.VMEM((STATE, inner), F32), pltpu.VMEM((8, inner), F32)],
        compiler_params=params(),
        cost_estimate=cost(1.5e9, 20e6),
        name="gate",
    )(mixed, proj_z, d_normed, sums, bc_act, cumul, gain, expander)

    adjoints = lax.all_gather(adjoint_packed, "seq")
    w_out_grad = dot(normed_out, piece, TN)
    w_z_grad = dot(normed_in, grad_z, TN)
    w_out_sum = lax.psum(w_out_grad.astype(BF16), "seq")
    w_z_sum = lax.psum(w_z_grad.astype(BF16), "seq")
    out_part = lax.psum_scatter(
        dot(normed_out, w_out).astype(BF16), "head", scatter_dimension=0, tiled=True
    )
    hidden_own = lax.dynamic_slice_in_dim(hidden_in, first_row, own_rows, 0).astype(F32)
    output = (hidden_own + out_part.astype(F32)).astype(BF16)
    adjoint_in = jnp.sum(weight_back[:, None, :] * adjoints.astype(F32), 0)

    def rows_before(width_here, block=0):
        per = CHUNK // 16
        return pl.BlockSpec(
            (16, width_here), lambda step: (jnp.maximum(behind(step) * per - 1, 0), block)
        )

    constants = (conv_x, bias_x, conv_bc_all, bias_bc_all, dt_bias_row, rate, skip, skip_heads, expander)
    grad_x, grad_bc, grad_dt, first_x, first_bc, conv_x_sums, conv_bc_sums, head_sums = pl.pallas_call(
        backward_kernel,
        grid=(chunks,),
        in_specs=[
            wide_r, rows_before(inner), pair_r, rows_before(2 * STATE), lanes_r,
            whole(edge_x), whole(edge_bc), pair_r, lanes_r, lanes_r, wide_r, wide_r,
            pl.BlockSpec((1, STATE, inner), lambda step: (behind(step), 0, 0)),
            whole(final_state), whole(adjoint_in),
        ]
        + [whole(a) for a in constants],
        out_specs=[wide_r, pair_r, lanes_r]
        + [
            pl.BlockSpec((8, width_here), lambda step: (0, 0))
            for width_here in (inner, 2 * STATE, inner, 2 * STATE, LANES)
        ],
        out_shape=[
            shape((tokens, inner), BF16),
            shape((tokens, 2 * STATE), BF16),
            shape((tokens, LANES), BF16),
        ]
        + [shape((8, width_here), F32) for width_here in (inner, 2 * STATE, inner, 2 * STATE, LANES)],
        scratch_shapes=[
            pltpu.VMEM((CHUNK + 8, inner), F32),
            pltpu.VMEM((CHUNK + 8, 2 * STATE), F32),
            pltpu.VMEM((CHUNK + 8, inner), F32),
            pltpu.VMEM((CHUNK + 8, 2 * STATE), F32),
            pltpu.VMEM((STATE, inner), F32),
            pltpu.VMEM((STATE, inner), BF16),
            pltpu.VMEM((3, HALF, HALF), F32),
            pltpu.VMEM((CHUNK, 2 * CHUNK), BF16),
            pltpu.VMEM((3, HALF, HALF), F32),
            pltpu.VMEM((CHUNK, LANES), F32),
            pltpu.VMEM((CHUNK, LANES), F32),
        ],
        compiler_params=params(),
        cost_estimate=cost(25e9, 25e6),
        name="backward_scan",
    )(
        proj_x, proj_x, proj_bc, proj_bc, proj_dt, edge_x, edge_bc, bc_act, steps, cumul, mixed, d_mixed,
        states, final_state, adjoint_in, *constants,
    )

    next_x, next_bc = from_behind((first_x, first_bc), "seq", -1)

    def close_edge(grad, taps, following):
        rows = []
        for row in range(CONV - 1):
            rows.append(
                sum(
                    taps[tap] * following[row + CONV - 1 - tap - (CONV - 1)]
                    for tap in range(CONV - 1)
                    if row + CONV - 1 - tap - (CONV - 1) >= 0
                )
            )
        extra = jnp.concatenate([jnp.zeros((16 - (CONV - 1), grad.shape[1]), F32), jnp.stack(rows)], 0)
        ending = (grad[-16:].astype(F32) + extra).astype(BF16)
        return lax.dynamic_update_slice(grad, ending, (tokens - 16, 0))

    grad_x = close_edge(grad_x, conv_x, next_x)
    grad_bc = close_edge(grad_bc, conv_bc_all, next_bc)

    w_x_grad = dot(normed_in, grad_x, TN)
    w_bc_grad = dot(normed_in, grad_bc, TN)
    w_dt_grad = dot(normed_in, grad_dt, TN)[:, 0:heads_here]
    d_rows = dot(grad_z, w_z, NT) + dot(grad_x, w_x, NT)
    d_rows = d_rows + dot(grad_bc, w_bc_all, NT) + dot(grad_dt, w_dt_wide, NT)
    d_normed_rows = lax.psum_scatter(
        d_rows.astype(BF16), "head", scatter_dimension=0, tiled=True
    ).astype(F32)
    w_x_sum = lax.psum(w_x_grad.astype(BF16), "seq")

    def own_states(partial):
        rows = partial.shape[0]
        parts = partial.reshape(rows, 2, -1, states_here).transpose(2, 0, 1, 3)
        return lax.psum_scatter(parts, "head", scatter_dimension=0, tiled=False)

    w_bc_own = own_states(w_bc_grad.astype(BF16))
    conv_bc_own = own_states(conv_bc_sums[0 : CONV + 1])

    inverse = lax.rsqrt(jnp.mean(hidden_own * hidden_own, -1, keepdims=True) + EPSILON)
    weighted = d_normed_rows * norm_gain
    dots = jnp.sum(weighted * hidden_own, -1, keepdims=True)
    input_grad = (
        out_grad.astype(F32)
        + inverse * weighted
        - hidden_own * (inverse * inverse * inverse * dots / width)
    )
    gain_part = jnp.sum(d_normed_rows * hidden_own * inverse, 0)
    norm_gain_grad = lax.psum(gain_part, ("seq", "head"))
    w_bc_sum, w_dt_sum = lax.psum((w_bc_own, w_dt_grad.astype(BF16)), "seq")
    conv_x_all, conv_bc_sum, head_all, gate_gain_grad = lax.psum(
        (conv_x_sums[0 : CONV + 1], conv_bc_own, head_sums[0:3, 0:heads_here], gain_grad[0]), "seq"
    )
    return (
        output,
        input_grad,
        norm_gain_grad,
        w_z_sum.astype(F32),
        w_x_sum.astype(F32),
        w_bc_sum.astype(F32),
        w_dt_sum.astype(F32),
        conv_x_all[0:CONV],
        conv_x_all[CONV],
        conv_bc_sum[0:CONV],
        conv_bc_sum[CONV],
        head_all[0],
        head_all[1],
        head_all[2],
        gate_gain_grad,
        w_out_sum.astype(F32),
    )


def solution(mesh):
    placed = (
        P("seq", None),
        P(),
        P(None, "head"),
        P(None, "head"),
        P(None, None, "head"),
        P(None, "head"),
        P(None, "head"),
        P("head"),
        P(None, None, "head"),
        P(None, "head"),
        P("head"),
        P("head"),
        P("head"),
        P("head"),
        P("head", None),
        P(("seq", "head"), None),
    )
    return jax.shard_map(
        per_device,
        mesh=mesh,
        in_specs=placed,
        out_specs=(
            P(("seq", "head"), None),
            P(("seq", "head"), None),
            P(),
            P(None, "head"),
            P(None, "head"),
            P(None, None, "head"),
            P(None, "head"),
            P(None, "head"),
            P("head"),
            P(None, None, "head"),
            P(None, "head"),
            P("head"),
            P("head"),
            P("head"),
            P("head"),
            P("head", None),
        ),
        check_vma=False,
    )
```
